256 devices in a mesh: grid: 64 (over y, x, z_lo, core), rep: 4 (over z_hi).
Axes of the slice: x: 4, y: 4, z: 8 (z_hi: 4, z_lo: 2; z = z_hi * 2 + z_lo), core: 2. Of those that a mesh axis runs over, the one named last changes fastest.
Arguments:
- amplitudes: bfloat16 [2, 832, 13312], P(None, 'grid', 'rep'), may hold values from -6 to 6
- integrals: bfloat16 [8, 13312, 13312], P(None, 'grid', 'rep'), may hold values from -0.0546875 to 0.0546875
- virt_size: int32 [8], replicated, may hold values from 60 to 208, as said below
- slab: int32 [2], replicated, may hold values from 0 to 127
Outputs:
- residual: float32 [2, 832, 13312], P(None, 'grid', 'rep')
The draws below stay inside these ranges and needn't reach their ends.
Inputs may be any that keep to these rules, and one draw needn't show every extreme that they name: `virt_size`: the sizes sum to 832; exactly one symmetry block holds 208 virtual orbitals, all others fewer.
All inputs are finite; a program needn't handle non-finite values.
Results may differ from the reference program's by a relative error of at most 0.0003.
Values may be sent and summed in bfloat16 or wider, within the bound.
A program may use at most 256 MiB of HBM per device.

```python
import jax
import jax.numpy as jnp
from jax import lax

NIRREP = 8
O = 128
V = 832
I = 2
PP = 13312


def draw_virt_size(key, part):
    key = jax.random.fold_in(key, 11)
    key_delta, key_order, key_big = jax.random.split(key, 3)
    largest = V // 4
    middle = (V - largest) // (NIRREP - 1)
    leftover = V - largest - middle * (NIRREP - 1)
    spread = V // 28
    delta = jax.random.randint(key_delta, (3,), 1 - spread, spread).astype(jnp.int32)
    others = middle + jnp.concatenate([delta, -delta, jnp.zeros((NIRREP - 7,), jnp.int32)])
    extra = jnp.where(jnp.arange(NIRREP - 1, dtype=jnp.int32) == 0, leftover, 0).astype(jnp.int32)
    others = (others + extra)[jax.random.permutation(key_order, NIRREP - 1)]
    where_big = jax.random.randint(key_big, (), 0, NIRREP).astype(jnp.int32)
    labels = jnp.arange(NIRREP, dtype=jnp.int32)
    position = jnp.clip(labels - (labels > where_big).astype(jnp.int32), 0, NIRREP - 2)
    return jnp.where(labels == where_big, largest, others[position]).astype(jnp.int32)


def shard_levels(stream_key, extent, cuts, low, high):
    gain, own = 1.0, jax.random.fold_in(stream_key, 6)
    for dim, shards_of in cuts:
        draws = jnp.exp(jax.random.uniform(jax.random.fold_in(own, dim), (shards_of,), jnp.float32, low / len(cuts), high / len(cuts)))
        gain = gain * jnp.repeat(draws, extent[dim] // shards_of).reshape([-1 if axis == dim else 1 for axis in range(len(extent))])
    return gain


def gaussian(key, extent, deviation, bound, shards=(), held_as=jnp.bfloat16):
    factor_of = shard_levels(key, extent, shards, -0.22, 0.18) if shards else 1.0
    values = jax.random.normal(key, extent, jnp.float32) * deviation * factor_of
    return jnp.minimum(jnp.maximum(values, -bound), bound).astype(held_as)


def setup_inputs(seed: int = 0) -> dict:
    keys = jax.random.split(jax.random.key(seed), 5)
    amplitudes = gaussian(keys[0], (I, V, PP), 1.0, 6.0, ((1, 64), (2, 4)))
    integrals = gaussian(keys[1], (NIRREP, PP, PP), PP ** -0.5, 0.0546875, ((1, 64), (2, 4)))
    virt_size = draw_virt_size(jax.random.fold_in(keys[4], 71), 0)
    slab = jax.random.randint(keys[3], (I,), 0, O).astype(jnp.int32)
    return dict(amplitudes=amplitudes, integrals=integrals, virt_size=virt_size, slab=slab)


def reference(amplitudes, integrals, virt_size, slab):
    occ_irrep = (slab // (O // NIRREP)).astype(jnp.int32)
    offsets = (jnp.cumsum(virt_size) - virt_size).astype(jnp.int32)
    window = V // 4
    row_index = jnp.arange(window, dtype=jnp.int32)[:, None]
    running = jnp.zeros((I, V, PP), jnp.float32)

    def visit(running, irrep_a):
        first_row = offsets[irrep_a]
        anchor = jnp.minimum(first_row, V - window).astype(jnp.int32)
        position = anchor + row_index
        inside = (position >= first_row) & (position < first_row + virt_size[irrep_a])
        for member in range(I):
            pair_irrep = jnp.bitwise_xor(occ_irrep[member], irrep_a).astype(jnp.int32)
            block_w = lax.dynamic_index_in_dim(integrals, pair_irrep, 0, keepdims=False)
            window_rows = lax.dynamic_slice_in_dim(amplitudes[member], anchor, window, 0)
            product = jnp.dot(window_rows, block_w.T, preferred_element_type=jnp.float32)
            product = jnp.where(inside, product, jnp.zeros_like(product))
            current = lax.dynamic_slice(running, (jnp.int32(member), anchor, jnp.int32(0)), (1, window, PP))
            running = lax.dynamic_update_slice(running, current + product[None], (jnp.int32(member), anchor, jnp.int32(0)))
        return running, None

    running, _ = lax.scan(visit, running, jnp.arange(NIRREP, dtype=jnp.int32))
    return running
```

```python
import functools

import jax
import jax.numpy as jnp
from jax import lax
from jax.experimental import pallas as pl
from jax.experimental.pallas import tpu as pltpu
from jax.sharding import PartitionSpec as P

NIRREP = 8
O = 128
RING = 4
K = 3328
Q = 208
ROWS = 13
PAD = 16
QUAD = 4
PIECE = QUAD * PAD
LANES = 256
DEPTH = 256
STEPS = 32700.0
MESH = pl.DeviceIdType.MESH


def turn(o):
    return o + o // 2 - 2 * (o // 3)


def encode(value, wide):
    peak = jnp.max(jnp.abs(value), axis=1, keepdims=True)
    level = jnp.ceil(jnp.log2(jnp.maximum(peak, 1e-30)) + 0.01)
    wide[:, :Q] = jnp.round(value * (jnp.exp2(-level) * STEPS))
    wide[:, Q:] = jnp.broadcast_to(level, (value.shape[0], LANES - Q))
    return wide[...].astype(jnp.int32).astype(jnp.int16)


def decode(coded):
    value = coded.astype(jnp.int32).astype(jnp.float32)
    return value * (jnp.exp2(value[:, Q:Q + 1]) * (1.0 / STEPS))


def kernel(
    slab_ref, virt_ref, amp_ref, w_hbm, out_ref,
    buf, w_ref, wide, stage, inbox, total, final,
    w_sem, recv_sem, send_sem, pair_sem,
    part_send, part_recv, sum_send, sum_recv, step_sem, far_sem,
):
    g = lax.axis_index("grid")
    r = lax.axis_index("rep")
    c = g % 2
    zl = (g // 2) % 2
    x = (g // 4) % RING
    y = g // 16

    def grid_of(yy, xx, zz, cc):
        return ((yy * RING + xx) * 2 + zz) * 2 + cc

    def chip_of(m, a, b):
        return b + m * (a - b), a + m * (b - a)

    a0 = (x, y)
    b0 = (y, x)

    def place(m, ob, oa):
        pa = (x + m * (y - x) + turn(oa)) % RING
        pb = (y + m * (x - y) + turn(ob)) % RING
        return chip_of(m, pa, pb)

    def neighbour(m, da, db):
        na = (x + m * (y - x) + da + RING) % RING
        nb = (y + m * (x - y) + db + RING) % RING
        yy, xx = chip_of(m, na, nb)
        return grid_of(yy, xx, zl, c)

    sibling = grid_of(y, x, zl, 1 - c)
    partner = grid_of(y, x, 1 - zl, c)

    barrier = pltpu.get_barrier_semaphore()
    near = [sibling, partner] + [neighbour(0, da, db) for da, db in ((1, 0), (-1, 0), (0, 1), (0, -1))]
    for n in near:
        pl.semaphore_signal(barrier, inc=1, device_id=(n, r), device_id_type=MESH)
    beyond = (grid_of(y, x, 1 - zl, c), (r + 2 * zl + 3) % 4)
    pl.semaphore_signal(barrier, inc=1, device_id=beyond, device_id_type=MESH)

    w_copy = pltpu.make_async_copy(w_hbm, w_ref, w_sem)
    w_copy.start()
    mine = y * RING + x
    for m in range(2):
        buf[m, mine, zl * 2 + c] = jnp.zeros((PAD, K), jnp.bfloat16)
        buf[m, mine, zl * 2 + c, :ROWS, :] = amp_ref[m]

    pl.semaphore_wait(barrier, len(near) + 1)
    pl.semaphore_signal(step_sem, inc=1, device_id=(partner, r), device_id_type=MESH)
    pl.semaphore_signal(step_sem, inc=1, device_id=beyond, device_id_type=MESH)

    def block_copy(m, pos, z, cc, sem, target):
        block = buf.at[m, pos, z * 2 + cc]
        return pltpu.make_async_remote_copy(
            src_ref=block, dst_ref=block, send_sem=sem, recv_sem=recv_sem.at[m, pos, z * 2 + cc],
            device_id=(target, r), device_id_type=MESH,
        )

    def arrived(m, pos, z, cc):
        block_copy(m, pos, z, cc, pair_sem.at[0], sibling).wait_recv()

    def do(copy, starting):
        if starting:
            copy.start()
        else:
            copy.wait_send()

    def own_pair(m, starting):
        do(block_copy(m, mine, zl, c, pair_sem.at[m], partner), starting)

    def relay(m, ob, oa, phase, starting):
        yy, xx = place(m, ob, oa)
        pos = yy * RING + xx
        for z in range(2):
            if starting:
                if phase == 0:
                    @pl.when((oa > 0) | (zl != z))
                    def _():
                        arrived(m, pos, z, c)
                else:
                    arrived(m, pos, z, c)

            def send(which, target):
                do(block_copy(m, pos, z, c, send_sem.at[m, pos, z, which], target), starting)

            if phase == 0:
                send(1, neighbour(m, 0, 1))
                send(2, neighbour(m, 0, -1))
                up = (oa == 0) if z == 0 else ((oa == 0) | (oa == 2))
                down = ((oa == 0) | (oa == 1)) if z == 0 else (oa == 0)

                @pl.when(up)
                def _():
                    send(3, neighbour(m, 1, 0))

                @pl.when(down)
                def _():
                    send(4, neighbour(m, -1, 0))
            elif phase == 1:
                if z == 0:
                    @pl.when(ob == 1)
                    def _():
                        send(2, neighbour(m, 0, -1))
                else:
                    @pl.when(ob == 2)
                    def _():
                        send(1, neighbour(m, 0, 1))
            send(0, sibling)

    row = lax.broadcasted_iota(jnp.int32, (PIECE, 1), 0)
    row_a = (row // PAD) * ROWS + row % PAD

    def part_copy(m, pos, yy, xx):
        return pltpu.make_async_remote_copy(
            src_ref=stage.at[m, pos], dst_ref=inbox.at[m, xx, r],
            send_sem=part_send.at[m, pos], recv_sem=part_recv.at[m, xx, r],
            device_id=(g, yy), device_id_type=MESH,
        )

    def compute(m, ob, oa):
        yy, xx = place(m, ob, oa)
        pos = yy * RING + xx
        for z in range(2):
            arrived(m, pos, z, 1 - c)
        first = pos * (QUAD * ROWS)
        last = first + QUAD * ROWS - 1
        low = jnp.int32(-1)
        high = jnp.int32(-1)
        offset = jnp.int32(0)
        edge = jnp.int32(0)
        for h in range(NIRREP):
            low = low + (offset <= first).astype(jnp.int32)
            high = high + (offset <= last).astype(jnp.int32)
            edge = jnp.where(offset <= last, offset, edge)
            offset = offset + virt_ref[h]
        occ = slab_ref[m] // (O // NIRREP)
        pair_low = low ^ occ
        pair_high = high ^ occ
        acc_low = jnp.zeros((PIECE, Q), jnp.float32)
        acc_high = jnp.zeros((PIECE, Q), jnp.float32)
        for k in range(0, K, DEPTH):
            left = buf[m, pos, :, :, k:k + DEPTH].reshape(PIECE, DEPTH)
            for which in range(2):
                right = w_ref[pair_high if which else pair_low, :, k:k + DEPTH]
                term = lax.dot_general(left, right, (((1,), (1,)), ((), ())), preferred_element_type=jnp.float32)
                if which:
                    acc_high = acc_high + term
                else:
                    acc_low = acc_low + term
        stage[m, pos] = encode(jnp.where(row_a + first >= edge, acc_high, acc_low), wide)

        @pl.when(yy != r)
        def _():
            part_copy(m, pos, yy, xx).start()

    def part_sent(m, ob, oa):
        yy, xx = place(m, ob, oa)

        @pl.when(yy != r)
        def _():
            part_copy(m, yy * RING + xx, yy, xx).wait_send()

    def sum_copy(m, xx, s):
        return pltpu.make_async_remote_copy(
            src_ref=total.at[m, xx, pl.ds(s * PAD, PAD)], dst_ref=final.at[m, g % 16],
            send_sem=sum_send.at[m, xx, s], recv_sem=sum_recv.at[m, g % 16],
            device_id=((r * RING + xx) * 4 + s, y), device_id_type=MESH,
        )

    def reduce(m, ob, oa):
        yy, xx = place(m, ob, oa)

        @pl.when(yy == r)
        def _():
            value = decode(stage[m, yy * RING + xx])
            for d in (1, 2, 3):
                src = (r + d) % 4
                pltpu.make_async_remote_copy(
                    src_ref=stage.at[m, 0], dst_ref=inbox.at[m, xx, src],
                    send_sem=part_send.at[m, 0], recv_sem=part_recv.at[m, xx, src],
                    device_id=(g, src), device_id_type=MESH,
                ).wait_recv()
                value = value + decode(inbox[m, xx, src])
            total[m, xx] = encode(value[:, :Q], wide)

            def ship(s, _):
                here = (y == r) & ((r * RING + xx) * 4 + s == g)

                @pl.when(here)
                def _():
                    final[m, g % 16] = total[m, xx, pl.ds(pl.multiple_of(s * PAD, PAD), PAD)]

                @pl.when(jnp.logical_not(here))
                def _():
                    sum_copy(m, xx, s).start()
                return 0

            lax.fori_loop(0, QUAD, ship, 0)

    for m in range(2):
        own_pair(m, True)

    def phase0(oa, _):
        for m in range(2):
            relay(m, 0, oa, 0, True)
        return 0

    lax.fori_loop(0, 4, phase0, 0)
    pl.semaphore_wait(step_sem, 2)
    for d in (1, 3):
        pl.semaphore_signal(far_sem, inc=1, device_id=(g, (r + d) % 4), device_id_type=MESH)
    w_copy.wait()
    pl.semaphore_wait(far_sem, 2)

    def reduce1(i):
        reduce(i % 2, 0, i // 2)
        for m in range(2):
            reduce(m, 1 + i % 2, i // 2)

    def phase1(i, _):
        ob, oa = 1 + i % 2, i // 2
        for m in range(2):
            relay(m, ob, oa, 1, True)

        @pl.when(i >= 2)
        def _():
            reduce1(i - 2)

        compute(i % 2, 0, i // 2)
        for m in range(2):
            compute(m, ob, oa)
        return 0

    lax.fori_loop(0, 8, phase1, 0)

    def phase2(oa, _):
        for m in range(2):
            relay(m, 3, oa, 2, True)

        @pl.when(oa < 2)
        def _():
            reduce1(oa + 6)

        @pl.when(oa >= 2)
        def _():
            for m in range(2):
                reduce(m, 3, oa - 2)

        for m in range(2):
            compute(m, 3, oa)
        return 0

    lax.fori_loop(0, 4, phase2, 0)
    for oa in (2, 3):
        for m in range(2):
            reduce(m, 3, oa)

    def done0(oa, _):
        for m in range(2):
            relay(m, 0, oa, 0, False)
            part_sent(m, 0, oa)
        return 0

    def done1(i, _):
        for m in range(2):
            relay(m, 1 + i % 2, i // 2, 1, False)
            part_sent(m, 1 + i % 2, i // 2)
        return 0

    def done2(oa, _):
        for m in range(2):
            relay(m, 3, oa, 2, False)
            part_sent(m, 3, oa)
        return 0

    for m in range(2):
        own_pair(m, False)
    lax.fori_loop(0, 4, done0, 0)
    lax.fori_loop(0, 8, done1, 0)
    lax.fori_loop(0, 4, done2, 0)

    def landed(k, _):
        @pl.when((y != r) | (r * 16 + k != g))
        def _():
            for m in range(2):
                pltpu.make_async_remote_copy(
                    src_ref=total.at[m, 0, pl.ds(0, PAD)], dst_ref=final.at[m, k],
                    send_sem=sum_send.at[m, 0, 0], recv_sem=sum_recv.at[m, k],
                    device_id=(r * 16 + k, y), device_id_type=MESH,
                ).wait_recv()
        return 0

    lax.fori_loop(0, 16, landed, 0)

    def shipped(t, _):
        xx, s = t // QUAD, t % QUAD

        @pl.when((y != r) | ((r * RING + xx) * 4 + s != g))
        def _():
            for m in range(2):
                sum_copy(m, xx, s).wait_send()
        return 0

    lax.fori_loop(0, 16, shipped, 0)
    for m in range(2):
        for k in range(16):
            out_ref[m, :, k * Q:(k + 1) * Q] = decode(final[m, k])[:ROWS, :Q]


def per_device(amplitudes, integrals, virt_size, slab):
    smem = pl.BlockSpec(memory_space=pltpu.SMEM)
    vmem = pl.BlockSpec(memory_space=pltpu.VMEM)
    dma = pltpu.SemaphoreType.DMA
    return pl.pallas_call(
        kernel,
        out_shape=jax.ShapeDtypeStruct((2, ROWS, K), jnp.float32),
        in_specs=[smem, smem, vmem, pl.BlockSpec(memory_space=pl.ANY)],
        out_specs=vmem,
        scratch_shapes=[
            pltpu.VMEM((2, 16, QUAD, PAD, K), jnp.bfloat16),
            pltpu.VMEM((NIRREP, Q, K), jnp.bfloat16),
            pltpu.VMEM((PIECE, LANES), jnp.float32),
            pltpu.VMEM((2, 16, PIECE, LANES), jnp.int16),
            pltpu.VMEM((2, 4, 4, PIECE, LANES), jnp.int16),
            pltpu.VMEM((2, 4, PIECE, LANES), jnp.int16),
            pltpu.VMEM((2, 16, PAD, LANES), jnp.int16),
            dma,
            dma((2, 16, 4)),
            dma((2, 16, 2, 5)),
            dma((2,)),
            dma((2, 16)),
            dma((2, 4, 4)),
            dma((2, 4, 4)),
            dma((2, 16)),
            pltpu.SemaphoreType.REGULAR,
            pltpu.SemaphoreType.REGULAR,
        ],
        compiler_params=pltpu.CompilerParams(
            collective_id=0, has_side_effects=True, vmem_limit_bytes=56 * 1024 * 1024
        ),
        cost_estimate=pl.CostEstimate(flops=4_600_000_000, bytes_accessed=12_000_000, transcendentals=0),
    )(slab, virt_size, amplitudes, integrals)


def solution(mesh):
    return jax.shard_map(
        per_device,
        mesh=mesh,
        in_specs=(P(None, "grid", "rep"), P(None, "grid", "rep"), P(), P()),
        out_specs=P(None, "grid", "rep"),
        check_vma=False,
    )
```

```python
import jax
import jax.numpy as jnp
from jax import lax
from jax.experimental import pallas as pl
from jax.experimental.pallas import tpu as pltpu
from jax.sharding import PartitionSpec as P

NIRREP = 8
O = 128
RING = 4
K = 3328
Q = 208
ROWS = 13
PAD = 16
QUAD = 4
PIECE = QUAD * PAD
LANES = 256
DEPTH = 256
MAIN = 2816
TAIL = K - MAIN
SPARE = PAD - ROWS
FOLDS = 5
STEPS = 32700.0
TURN = (0, 1, 3, 2)
MESH = pl.DeviceIdType.MESH


def encode(value, wide):
    peak = jnp.max(jnp.abs(value), axis=1, keepdims=True)
    level = jnp.ceil(jnp.log2(jnp.maximum(peak, 1e-30)) + 0.01)
    wide[:, :Q] = jnp.round(value * (jnp.exp2(-level) * STEPS))
    wide[:, Q:] = jnp.broadcast_to(level, (value.shape[0], LANES - Q))
    return wide[...].astype(jnp.int32).astype(jnp.int16)


def decode(coded):
    value = coded.astype(jnp.int32).astype(jnp.float32)
    return value * (jnp.exp2(value[:, Q:Q + 1]) * (1.0 / STEPS))


def kernel(
    slab_ref, virt_ref, amp_ref, w_hbm, out_ref,
    buf, w_ref, fold, tail, wide, stage, inbox, total, final, low_tab, high_tab, edge_tab,
    w_sem, recv_sem, side_sem, side_send, major_send, minor_send, extra_send,
    part_send, part_recv, sum_send, sum_recv, step_sem, far_sem,
):
    g = lax.axis_index("grid")
    r = lax.axis_index("rep")
    c = lax.rem(g, 2)
    zl = lax.rem(lax.div(g, 2), 2)
    x = lax.rem(lax.div(g, 4), RING)
    y = lax.div(g, 16)
    within = lax.rem(g, 16)
    xs = [lax.rem(x + d, RING) for d in range(RING)]
    ys = [lax.rem(y + d, RING) for d in range(RING)]

    def grid_of(yy, xx, zz, cc):
        return ((yy * RING + xx) * 2 + zz) * 2 + cc

    x_up, x_down = grid_of(y, xs[1], zl, c), grid_of(y, xs[3], zl, c)
    y_up, y_down = grid_of(ys[1], x, zl, c), grid_of(ys[3], x, zl, c)
    sibling = grid_of(y, x, zl, 1 - c)
    partner = grid_of(y, x, 1 - zl, c)
    beyond = (grid_of(y, x, 1 - zl, c), lax.rem(r + 2 * zl + 3, 4))
    minor_up, minor_down = (x_up, y_up), (x_down, y_down)
    major_up, major_down = (y_up, x_up), (y_down, x_down)
    mine = y * RING + x

    barrier = pltpu.get_barrier_semaphore()
    near = [sibling, partner, x_up, x_down, y_up, y_down]
    for n in near:
        pl.semaphore_signal(barrier, inc=1, device_id=(n, r), device_id_type=MESH)
    pl.semaphore_signal(barrier, inc=1, device_id=beyond, device_id_type=MESH)

    w_copy = pltpu.make_async_copy(w_hbm, w_ref, w_sem)
    w_copy.start()
    for m in range(2):
        whole = amp_ref[:, m, :].astype(jnp.float32)
        fold[:ROWS, :] = whole[:, :MAIN]
        fold[ROWS:, FOLDS * TAIL:] = jnp.zeros((SPARE, MAIN - FOLDS * TAIL), jnp.float32)
        fold[ROWS + 1:, (FOLDS - 1) * TAIL:FOLDS * TAIL] = jnp.zeros((SPARE - 1, TAIL), jnp.float32)
        for j in range(FOLDS):
            n = min(SPARE, ROWS - SPARE * j)
            fold[ROWS:ROWS + n, j * TAIL:(j + 1) * TAIL] = whole[SPARE * j:SPARE * j + n, MAIN:]
        buf[m, mine, zl * 2 + c] = fold[...].astype(jnp.bfloat16)
    tail[...] = jnp.zeros_like(tail)

    def table(pos, _):
        first = pos * (QUAD * ROWS)
        last = first + QUAD * ROWS - 1
        low = jnp.int32(-1)
        high = jnp.int32(-1)
        offset = jnp.int32(0)
        edge = jnp.int32(0)
        for h in range(NIRREP):
            low = low + (offset <= first).astype(jnp.int32)
            high = high + (offset <= last).astype(jnp.int32)
            edge = jnp.where(offset <= last, offset, edge)
            offset = offset + virt_ref[h]
        low_tab[pos] = low
        high_tab[pos] = high
        edge_tab[pos] = edge - first
        return 0

    lax.fori_loop(0, 16, table, 0)
    occ = [slab_ref[m] // (O // NIRREP) for m in range(2)]

    pl.semaphore_wait(barrier, len(near) + 1)

    def block_copy(m, pos, z, cc, send, recv, target):
        block = buf.at[m, pos, z * 2 + cc]
        return pltpu.make_async_remote_copy(
            src_ref=block, dst_ref=block, send_sem=send, recv_sem=recv,
            device_id=(target, r), device_id_type=MESH,
        )

    def push(m, pos, z, sem, target):
        block_copy(m, pos, z, c, sem.at[m], recv_sem.at[m, pos, z], target).start()

    def cross(m, pos, z):
        block_copy(m, pos, z, c, side_send.at[m], side_sem.at[m, pos], sibling).start()

    def arrived(m, pos, z):
        block_copy(m, pos, z, c, side_send.at[m], recv_sem.at[m, pos, z], sibling).wait_recv()

    def spread(m, pos, z):
        push(m, pos, z, major_send, major_up[m])
        push(m, pos, z, major_send, major_down[m])

    def place(m, tb, pa):
        return (ys[tb], pa) if m == 0 else (pa, xs[tb])

    def where(m, tb, pa):
        yy, xx = place(m, tb, pa)
        return yy * RING + xx

    along = (xs, ys)
    for m in range(2):
        push(m, mine, zl, extra_send, partner)
    for m in range(2):
        push(m, mine, zl, minor_send, minor_up[m])
        push(m, mine, zl, minor_send, minor_down[m])
        spread(m, mine, zl)
        cross(m, mine, zl)
    pl.semaphore_signal(step_sem, inc=1, device_id=(partner, r), device_id_type=MESH)
    pl.semaphore_signal(step_sem, inc=1, device_id=beyond, device_id_type=MESH)
    for m in range(2):
        arrived(m, mine, 1 - zl)
        push(m, mine, 1 - zl, minor_send, minor_up[m])
        push(m, mine, 1 - zl, minor_send, minor_down[m])
        spread(m, mine, 1 - zl)
        cross(m, mine, 1 - zl)
    for z in range(2):
        for d in ((1, 3) if z == 0 else (3, 1)):
            for m in range(2):
                pos = where(m, 0, along[m][d])
                arrived(m, pos, z)
                if z == 0 and d == 1:
                    push(m, pos, z, extra_send, minor_down[m])
                if z == 1 and d == 3:
                    push(m, pos, z, extra_send, minor_up[m])
                spread(m, pos, z)
                cross(m, pos, z)
    for z in range(2):
        for m in range(2):
            pos = where(m, 0, along[m][2])
            arrived(m, pos, z)
            spread(m, pos, z)
            cross(m, pos, z)
    pl.semaphore_wait(step_sem, 2)
    for d in (1, 3):
        pl.semaphore_signal(far_sem, inc=1, device_id=(g, lax.rem(r + d, 4)), device_id_type=MESH)
    w_copy.wait()
    pl.semaphore_wait(far_sem, 2)

    row = lax.broadcasted_iota(jnp.int32, (PIECE, 1), 0)
    row_a = (row // PAD) * ROWS + row % PAD

    def part_copy(m, pos, yy, xx):
        return pltpu.make_async_remote_copy(
            src_ref=stage.at[m, pos], dst_ref=inbox.at[m, xx, r],
            send_sem=part_send.at[m], recv_sem=part_recv.at[m, xx],
            device_id=(g, yy), device_id_type=MESH,
        )

    def compute(m, tb, pa):
        yy, xx = place(m, tb, pa)
        pos = yy * RING + xx
        both = buf.at[m, pos, pl.ds(0, 2)]
        pltpu.make_async_remote_copy(
            src_ref=both, dst_ref=both, send_sem=side_send.at[m], recv_sem=side_sem.at[m, pos],
            device_id=(sibling, r), device_id_type=MESH,
        ).wait_recv()
        pair_low = low_tab[pos] ^ occ[m]
        pair_high = high_tab[pos] ^ occ[m]
        edge = edge_tab[pos]
        for s in range(QUAD):
            spill = buf[m, pos, s, :, :FOLDS * TAIL].astype(jnp.float32)
            for j in range(FOLDS):
                n = min(SPARE, ROWS - SPARE * j)
                start = s * PAD + SPARE * j
                tail[start:start + n, :] = spill[ROWS:ROWS + n, j * TAIL:(j + 1) * TAIL]
        acc_low = jnp.zeros((PIECE, Q), jnp.float32)
        acc_high = jnp.zeros((PIECE, Q), jnp.float32)
        for k in range(0, K, DEPTH):
            if k < MAIN:
                left = buf[m, pos, :, :, k:k + DEPTH].reshape(PIECE, DEPTH)
            else:
                left = tail[:, k - MAIN:k - MAIN + DEPTH].astype(jnp.bfloat16)
            for which in range(2):
                right = w_ref[pair_high if which else pair_low, :, k:k + DEPTH]
                term = lax.dot_general(left, right, (((1,), (1,)), ((), ())), preferred_element_type=jnp.float32)
                if which:
                    acc_high = acc_high + term
                else:
                    acc_low = acc_low + term
        stage[m, pos] = encode(jnp.where(row_a >= edge, acc_high, acc_low), wide)

        @pl.when(yy != r)
        def _():
            part_copy(m, pos, yy, xx).start()

    def sum_copy(m, xx, s):
        return pltpu.make_async_remote_copy(
            src_ref=total.at[m, xx, pl.ds(s * PAD, PAD)], dst_ref=final.at[m, within],
            send_sem=sum_send.at[m, xx], recv_sem=sum_recv.at[m],
            device_id=((r * RING + xx) * 4 + s, y), device_id_type=MESH,
        )

    def reduce(m, tb, pa):
        yy, xx = place(m, tb, pa)

        @pl.when(yy == r)
        def _():
            three = inbox.at[m, xx, pl.ds(0, 3)]
            pltpu.make_async_remote_copy(
                src_ref=three, dst_ref=three, send_sem=part_send.at[m], recv_sem=part_recv.at[m, xx],
                device_id=(g, lax.rem(r + 1, 4)), device_id_type=MESH,
            ).wait_recv()
            value = decode(stage[m, yy * RING + xx])
            for d in (1, 2, 3):
                value = value + decode(inbox[m, xx, lax.rem(r + d, 4)])
            total[m, xx] = encode(value[:, :Q], wide)

            def ship(s, _):
                here = (y == r) & ((r * RING + xx) * 4 + s == g)

                @pl.when(here)
                def _():
                    final[m, within] = total[m, xx, pl.ds(pl.multiple_of(s * PAD, PAD), PAD)]

                @pl.when(jnp.logical_not(here))
                def _():
                    sum_copy(m, xx, s).start()
                return 0

            lax.fori_loop(0, QUAD, ship, 0)

    def relay(m, tb, pa):
        pos = where(m, tb, pa)
        for z in ((1, 0) if tb == 3 else (0, 1)):
            arrived(m, pos, z)
            if tb == 1 and z == 0:
                push(m, pos, z, major_send, major_down[m])
            if tb == 3 and z == 1:
                push(m, pos, z, major_send, major_up[m])
            cross(m, pos, z)

    def spots(oa):
        t = oa + lax.div(oa, 2) - 2 * lax.div(oa, 3)
        return lax.rem(x + t, RING), lax.rem(y + t, RING)

    def phase1(oa, _):
        pa = spots(oa)
        relay(0, 1, pa[0])
        compute(0, 0, pa[0])
        relay(1, 1, pa[1])
        relay(0, 3, pa[0])
        compute(1, 0, pa[1])
        relay(1, 3, pa[1])
        compute(0, 1, pa[0])
        compute(1, 1, pa[1])
        compute(0, 3, pa[0])
        compute(1, 3, pa[1])
        return 0

    lax.fori_loop(0, 4, phase1, 0)

    def phase2(oa, _):
        pa = spots(oa)
        relay(0, 2, pa[0])
        relay(1, 2, pa[1])
        for m in range(2):
            compute(m, 2, pa[m])
            for tb in (0, 1, 3):
                reduce(m, tb, pa[m])
        return 0

    lax.fori_loop(0, 4, phase2, 0)

    def finish(oa, _):
        pa = spots(oa)
        for m in range(2):
            reduce(m, 2, pa[m])
        return 0

    lax.fori_loop(0, 4, finish, 0)

    def wait_sent(ref, sem):
        pltpu.make_async_remote_copy(
            src_ref=ref, dst_ref=ref, send_sem=sem, recv_sem=sum_recv.at[0],
            device_id=(sibling, r), device_id_type=MESH,
        ).wait_send()

    for m in range(2):
        wait_sent(buf.at[m, pl.ds(0, 8)], side_send.at[m])
        wait_sent(buf.at[m, pl.ds(0, 6)], major_send.at[m])
        wait_sent(buf.at[m, 0], minor_send.at[m])
        wait_sent(buf.at[m, 0, pl.ds(0, 3)], extra_send.at[m])
        wait_sent(stage.at[m, pl.ds(0, 12)], part_send.at[m])
        for xx in range(RING):
            inside = (y == r) & (x == xx)

            @pl.when(inside)
            def _():
                wait_sent(total.at[m, xx, pl.ds(0, PIECE - PAD)], sum_send.at[m, xx])

            @pl.when(jnp.logical_not(inside))
            def _():
                wait_sent(total.at[m, xx], sum_send.at[m, xx])

        def landed(ref):
            pltpu.make_async_remote_copy(
                src_ref=ref, dst_ref=ref, send_sem=sum_send.at[m, 0], recv_sem=sum_recv.at[m],
                device_id=(sibling, r), device_id_type=MESH,
            ).wait_recv()

        @pl.when(y == r)
        def _():
            landed(final.at[m, pl.ds(0, 15)])

        @pl.when(y != r)
        def _():
            landed(final.at[m])
        for k in range(16):
            out_ref[:, m, k * Q:(k + 1) * Q] = decode(final[m, k])[:ROWS, :Q]


def per_device(amplitudes, integrals, virt_size, slab):
    smem = pl.BlockSpec(memory_space=pltpu.SMEM)
    vmem = pl.BlockSpec(memory_space=pltpu.VMEM)
    dma = pltpu.SemaphoreType.DMA
    out = pl.pallas_call(
        kernel,
        out_shape=jax.ShapeDtypeStruct((ROWS, 2, K), jnp.float32),
        in_specs=[smem, smem, vmem, pl.BlockSpec(memory_space=pl.ANY)],
        out_specs=vmem,
        scratch_shapes=[
            pltpu.VMEM((2, 16, QUAD, PAD, MAIN), jnp.bfloat16),
            pltpu.VMEM((NIRREP, Q, K), jnp.bfloat16),
            pltpu.VMEM((PAD, MAIN), jnp.float32),
            pltpu.VMEM((PIECE, TAIL), jnp.float32),
            pltpu.VMEM((PIECE, LANES), jnp.float32),
            pltpu.VMEM((2, 16, PIECE, LANES), jnp.int16),
            pltpu.VMEM((2, 4, 4, PIECE, LANES), jnp.int16),
            pltpu.VMEM((2, 4, PIECE, LANES), jnp.int16),
            pltpu.VMEM((2, 16, PAD, LANES), jnp.int16),
            pltpu.SMEM((16,), jnp.int32),
            pltpu.SMEM((16,), jnp.int32),
            pltpu.SMEM((16,), jnp.int32),
            dma,
            dma((2, 16, 2)),
            dma((2, 16)),
            dma((2,)),
            dma((2,)),
            dma((2,)),
            dma((2,)),
            dma((2,)),
            dma((2, 4)),
            dma((2, 4)),
            dma((2,)),
            pltpu.SemaphoreType.REGULAR,
            pltpu.SemaphoreType.REGULAR,
        ],
        compiler_params=pltpu.CompilerParams(
            collective_id=0, has_side_effects=True, vmem_limit_bytes=56 * 1024 * 1024
        ),
        cost_estimate=pl.CostEstimate(flops=4_600_000_000, bytes_accessed=12_000_000, transcendentals=0),
    )(slab, virt_size, jnp.transpose(amplitudes, (1, 0, 2)), integrals)
    return jnp.transpose(out, (1, 0, 2))


def solution(mesh):
    return jax.shard_map(
        per_device,
        mesh=mesh,
        in_specs=(P(None, "grid", "rep"), P(None, "grid", "rep"), P(), P()),
        out_specs=P(None, "grid", "rep"),
        check_vma=False,
    )
```

```python
import jax
import jax.numpy as jnp
from jax import lax
from jax.experimental import pallas as pl
from jax.experimental.pallas import tpu as pltpu
from jax.sharding import PartitionSpec as P

NIRREP = 8
O = 128
RING = 4
K = 3328
Q = 208
ROWS = 13
PAD = 16
QUAD = 4
PIECE = QUAD * PAD
LANES = 256
DEPTH = 256
MAIN = 2816
TAIL = K - MAIN
SPARE = PAD - ROWS
FOLDS = 5
STEPS = 32700.0
LAG = 4
MESH = pl.DeviceIdType.MESH


def encode(value, wide):
    peak = jnp.max(jnp.abs(value), axis=1, keepdims=True)
    level = jnp.ceil(jnp.log2(jnp.maximum(peak, 1e-30)) + 0.01)
    wide[:, :Q] = jnp.round(value * (jnp.exp2(-level) * STEPS))
    wide[:, Q:] = jnp.broadcast_to(level, (value.shape[0], LANES - Q))
    return wide[...].astype(jnp.int32).astype(jnp.int16)


def decode(coded):
    value = coded.astype(jnp.int32).astype(jnp.float32)
    return value * (jnp.exp2(value[:, Q:Q + 1]) * (1.0 / STEPS))


def kernel(
    slab_ref, virt_ref, amp_ref, w_hbm, out_ref,
    buf, w_ref, fold, tail, wide, stage, inbox, total, final, low_tab, high_tab, edge_tab,
    w_sem, recv_sem, side_sem, side_send, major_send, minor_send, extra_send,
    part_send, part_recv, sum_send, sum_recv, step_sem, far_sem,
):
    g = lax.axis_index("grid")
    r = lax.axis_index("rep")
    c = lax.rem(g, 2)
    zl = lax.rem(lax.div(g, 2), 2)
    x = lax.rem(lax.div(g, 4), RING)
    y = lax.div(g, 16)
    within = lax.rem(g, 16)
    xs = [lax.rem(x + d, RING) for d in range(RING)]
    ys = [lax.rem(y + d, RING) for d in range(RING)]

    def grid_of(yy, xx, zz, cc):
        return ((yy * RING + xx) * 2 + zz) * 2 + cc

    x_up, x_down = grid_of(y, xs[1], zl, c), grid_of(y, xs[3], zl, c)
    y_up, y_down = grid_of(ys[1], x, zl, c), grid_of(ys[3], x, zl, c)
    sibling = grid_of(y, x, zl, 1 - c)
    partner = grid_of(y, x, 1 - zl, c)
    beyond = (grid_of(y, x, 1 - zl, c), lax.rem(r + 2 * zl + 3, 4))
    minor_up, minor_down = (x_up, y_up), (x_down, y_down)
    major_up, major_down = (y_up, x_up), (y_down, x_down)
    mine = y * RING + x

    barrier = pltpu.get_barrier_semaphore()
    near = [sibling, partner, x_up, x_down, y_up, y_down]
    for n in near:
        pl.semaphore_signal(barrier, inc=1, device_id=(n, r), device_id_type=MESH)
    pl.semaphore_signal(barrier, inc=1, device_id=beyond, device_id_type=MESH)

    w_copy = pltpu.make_async_copy(w_hbm, w_ref, w_sem)
    w_copy.start()
    for m in range(2):
        whole = amp_ref[:, m, :].astype(jnp.float32)
        fold[:ROWS, :] = whole[:, :MAIN]
        fold[ROWS:, FOLDS * TAIL:] = jnp.zeros((SPARE, MAIN - FOLDS * TAIL), jnp.float32)
        fold[ROWS + 1:, (FOLDS - 1) * TAIL:FOLDS * TAIL] = jnp.zeros((SPARE - 1, TAIL), jnp.float32)
        for j in range(FOLDS):
            n = min(SPARE, ROWS - SPARE * j)
            fold[ROWS:ROWS + n, j * TAIL:(j + 1) * TAIL] = whole[SPARE * j:SPARE * j + n, MAIN:]
        buf[m, mine, c * 2 + zl] = fold[...].astype(jnp.bfloat16)
    tail[...] = jnp.zeros_like(tail)

    def table(pos, _):
        first = pos * (QUAD * ROWS)
        last = first + QUAD * ROWS - 1
        low = jnp.int32(-1)
        high = jnp.int32(-1)
        offset = jnp.int32(0)
        edge = jnp.int32(0)
        for h in range(NIRREP):
            low = low + (offset <= first).astype(jnp.int32)
            high = high + (offset <= last).astype(jnp.int32)
            edge = jnp.where(offset <= last, offset, edge)
            offset = offset + virt_ref[h]
        low_tab[pos] = low
        high_tab[pos] = high
        edge_tab[pos] = edge - first
        return 0

    lax.fori_loop(0, 16, table, 0)
    occ = [slab_ref[m] // (O // NIRREP) for m in range(2)]

    pl.semaphore_wait(barrier, len(near) + 1)

    def block_copy(m, pos, z, send, recv, target):
        block = buf.at[m, pos, pl.ds(2 * c, 2)] if z is None else buf.at[m, pos, c * 2 + z]
        return pltpu.make_async_remote_copy(
            src_ref=block, dst_ref=block, send_sem=send, recv_sem=recv,
            device_id=(target, r), device_id_type=MESH,
        )

    def push(m, pos, z, sem, target):
        block_copy(m, pos, z, sem.at[m], recv_sem.at[m, pos], target).start()

    def cross(m, pos):
        block_copy(m, pos, None, side_send.at[m], side_sem.at[m, pos], sibling).start()

    def arrived(m, pos, z):
        block_copy(m, pos, z, side_send.at[m], recv_sem.at[m, pos], sibling).wait_recv()

    def spread(m, pos, z):
        push(m, pos, z, major_send, major_up[m])
        push(m, pos, z, major_send, major_down[m])

    def place(m, tb, ta):
        db, da = (y, x) if m == 0 else (x, y)
        pb, pa = lax.rem(db + tb, RING), lax.rem(da + ta, RING)
        return (pb, pa) if m == 0 else (pa, pb)

    def take(m, tb, ta):
        yy, xx = place(m, tb, ta)
        pos = yy * RING + xx
        arrived(m, pos, None)

        @pl.when(tb == 0)
        def _():
            @pl.when(ta == 1)
            def _():
                push(m, pos, 0, extra_send, minor_down[m])

            @pl.when(ta == 3)
            def _():
                push(m, pos, 1, extra_send, minor_up[m])

            spread(m, pos, None)

        for side, target in ((1, major_down[m]), (3, major_up[m])):
            @pl.when((tb == side) & ((ta == 0) | (ta == 2)))
            def _():
                push(m, pos, side // 2, major_send, target)

            @pl.when((tb == side) & (ta == side))
            def _():
                push(m, pos, None, major_send, target)

        cross(m, pos)

    for m in range(2):
        push(m, mine, zl, extra_send, partner)
    for m in range(2):
        push(m, mine, zl, minor_send, minor_up[m])
        push(m, mine, zl, minor_send, minor_down[m])
        spread(m, mine, zl)
    pl.semaphore_signal(step_sem, inc=1, device_id=(partner, r), device_id_type=MESH)
    pl.semaphore_signal(step_sem, inc=1, device_id=beyond, device_id_type=MESH)
    for m in range(2):
        arrived(m, mine, 1 - zl)
        push(m, mine, 1 - zl, minor_send, minor_up[m])
        push(m, mine, 1 - zl, minor_send, minor_down[m])
        spread(m, mine, 1 - zl)
        cross(m, mine)
    pl.semaphore_wait(step_sem, 2)
    for d in (1, 3):
        pl.semaphore_signal(far_sem, inc=1, device_id=(g, lax.rem(r + d, 4)), device_id_type=MESH)
    w_copy.wait()
    pl.semaphore_wait(far_sem, 2)

    row = lax.broadcasted_iota(jnp.int32, (PIECE, 1), 0)
    part = row // PAD
    row_a = ((part % 2) * 2 + part // 2) * ROWS + row % PAD

    others = [lax.rem(r + d, 4) for d in (1, 2, 3)]

    def send_parts(step):
        for there in others:
            pltpu.make_async_remote_copy(
                src_ref=stage.at[there, pl.ds(2 * step, 2)], dst_ref=inbox.at[r, pl.ds(2 * step, 2)],
                send_sem=part_send, recv_sem=part_recv.at[step],
                device_id=(g, there), device_id_type=MESH,
            ).start()

    def compute(m, tb, ta, t):
        yy, xx = place(m, tb, ta)
        pos = yy * RING + xx
        pair = buf.at[m, pos, pl.ds(0, 2)]
        pltpu.make_async_remote_copy(
            src_ref=pair, dst_ref=pair, send_sem=side_send.at[m], recv_sem=side_sem.at[m, pos],
            device_id=(sibling, r), device_id_type=MESH,
        ).wait_recv()
        pair_low = low_tab[pos] ^ occ[m]
        pair_high = high_tab[pos] ^ occ[m]
        edge = edge_tab[pos]
        for s in range(QUAD):
            spill = buf[m, pos, s, :, :FOLDS * TAIL].astype(jnp.float32)
            for j in range(FOLDS):
                n = min(SPARE, ROWS - SPARE * j)
                start = s * PAD + SPARE * j
                tail[start:start + n, :] = spill[ROWS:ROWS + n, j * TAIL:(j + 1) * TAIL]
        acc_low = jnp.zeros((PIECE, Q), jnp.float32)
        acc_high = jnp.zeros((PIECE, Q), jnp.float32)
        for k in range(0, K, DEPTH):
            if k < MAIN:
                left = buf[m, pos, :, :, k:k + DEPTH].reshape(PIECE, DEPTH)
            else:
                left = tail[:, k - MAIN:k - MAIN + DEPTH].astype(jnp.bfloat16)
            for which in range(2):
                right = w_ref[pair_high if which else pair_low, :, k:k + DEPTH]
                term = lax.dot_general(left, right, (((1,), (1,)), ((), ())), preferred_element_type=jnp.float32)
                if which:
                    acc_high = acc_high + term
                else:
                    acc_low = acc_low + term
        coded = encode(jnp.where(row_a >= edge, acc_high, acc_low), wide.at[pl.ds(0, PIECE)])
        for there in range(4):
            stage[there, t] = coded[there * PAD:(there + 1) * PAD]

    alone = (y == r) & (c * 2 + zl == r)
    seat = lax.rem(r, 2) * 2 + lax.div(r, 2)

    def reduce(step, tb, ta):
        three = inbox.at[0, pl.ds(0, 6)]
        pltpu.make_async_remote_copy(
            src_ref=three, dst_ref=three, send_sem=part_send, recv_sem=part_recv.at[step],
            device_id=(g, others[0]), device_id_type=MESH,
        ).wait_recv()

        def load(ref, k):
            return decode(ref[k, pl.ds(2 * step, 2)].reshape(2 * PAD, LANES))

        value = load(stage, r)
        for there in others:
            value = value + load(inbox, there)
        coded = encode(value[:, :Q], wide.at[pl.ds(0, 2 * PAD)])
        total[pl.ds(2 * step, 2)] = coded.reshape(2, PAD, LANES)
        here = alone & (step == 0)
        for m in range(2):
            yy, xx = place(m, tb, ta)

            @pl.when(here)
            def _():
                final[m, within] = total[2 * step + m]

            @pl.when(jnp.logical_not(here))
            def _():
                pltpu.make_async_remote_copy(
                    src_ref=total.at[2 * step + m], dst_ref=final.at[m, within],
                    send_sem=sum_send.at[m], recv_sem=sum_recv.at[m],
                    device_id=((yy * RING + xx) * 4 + seat, y), device_id_type=MESH,
                ).start()

    order = (
        (0, 0), (0, 1), (0, 3), (1, 0), (3, 0), (0, 2), (1, 1), (3, 3),
        (1, 3), (3, 1), (2, 0), (1, 2), (3, 2), (2, 1), (2, 3), (2, 2),
    )

    def code(k, first, last):
        return sum(order[i][k] * 4 ** (i - first) for i in range(first, last))

    def work(step, state):
        tb, ta, cb, ca = state
        nb, na = lax.rem(cb, 4), lax.rem(ca, 4)
        for m in range(2):
            take(m, nb, na)
            compute(m, tb, ta, 2 * step + m)
        send_parts(step)
        return nb, na, lax.div(cb, 4), lax.div(ca, 4)

    def work_and_reduce(step, states):
        state, (rb, ra) = states
        state = work(step, state)
        reduce(step - LAG, lax.rem(rb, 4), lax.rem(ra, 4))
        return state, (lax.div(rb, 4), lax.div(ra, 4))

    def rest(step, old):
        rb, ra = old
        reduce(step, lax.rem(rb, 4), lax.rem(ra, 4))
        return lax.div(rb, 4), lax.div(ra, 4)

    zero = jnp.int32(0)
    state = (zero, zero, jnp.int32(code(0, 1, 16)), jnp.int32(code(1, 1, 16)))
    old = (jnp.int32(code(0, 0, 15 - LAG)), jnp.int32(code(1, 0, 15 - LAG)))
    state = lax.fori_loop(0, LAG, work, state)
    state, _ = lax.fori_loop(LAG, 15, work_and_reduce, (state, old))
    for m in range(2):
        compute(m, state[0], state[1], 30 + m)
    send_parts(15)
    left = (jnp.int32(code(0, 15 - LAG, 16)), jnp.int32(code(1, 15 - LAG, 16)))
    lax.fori_loop(15 - LAG, 16, rest, left)

    def wait_sent(ref, sem):
        pltpu.make_async_remote_copy(
            src_ref=ref, dst_ref=ref, send_sem=sem, recv_sem=sum_recv.at[0],
            device_id=(sibling, r), device_id_type=MESH,
        ).wait_send()

    wait_sent(stage.at[pl.ds(0, 3)], part_send)
    for m in range(2):
        wait_sent(buf.at[m, pl.ds(0, 8)], side_send.at[m])
        wait_sent(buf.at[m, pl.ds(0, 6)], major_send.at[m])
        wait_sent(buf.at[m, 0], minor_send.at[m])
        wait_sent(buf.at[m, 0, pl.ds(0, 3)], extra_send.at[m])

        def settle(ref):
            copy = pltpu.make_async_remote_copy(
                src_ref=ref, dst_ref=ref, send_sem=sum_send.at[m], recv_sem=sum_recv.at[m],
                device_id=(sibling, r), device_id_type=MESH,
            )
            copy.wait_send()
            copy.wait_recv()

        @pl.when(alone)
        def _():
            settle(final.at[m, pl.ds(0, 15)])

        @pl.when(jnp.logical_not(alone))
        def _():
            settle(final.at[m])
        for k in range(16):
            out_ref[:, m, k * Q:(k + 1) * Q] = decode(final[m, k])[:ROWS, :Q]


def per_device(amplitudes, integrals, virt_size, slab):
    smem = pl.BlockSpec(memory_space=pltpu.SMEM)
    vmem = pl.BlockSpec(memory_space=pltpu.VMEM)
    dma = pltpu.SemaphoreType.DMA
    out = pl.pallas_call(
        kernel,
        out_shape=jax.ShapeDtypeStruct((ROWS, 2, K), jnp.float32),
        in_specs=[smem, smem, vmem, pl.BlockSpec(memory_space=pl.ANY)],
        out_specs=vmem,
        scratch_shapes=[
            pltpu.VMEM((2, 16, QUAD, PAD, MAIN), jnp.bfloat16),
            pltpu.VMEM((NIRREP, Q, K), jnp.bfloat16),
            pltpu.VMEM((PAD, MAIN), jnp.float32),
            pltpu.VMEM((PIECE, TAIL), jnp.float32),
            pltpu.VMEM((PIECE, LANES), jnp.float32),
            pltpu.VMEM((4, 32, PAD, LANES), jnp.int16),
            pltpu.VMEM((4, 32, PAD, LANES), jnp.int16),
            pltpu.VMEM((32, PAD, LANES), jnp.int16),
            pltpu.VMEM((2, 16, PAD, LANES), jnp.int16),
            pltpu.SMEM((16,), jnp.int32),
            pltpu.SMEM((16,), jnp.int32),
            pltpu.SMEM((16,), jnp.int32),
            dma,
            dma((2, 16)),
            dma((2, 16)),
            dma((2,)),
            dma((2,)),
            dma((2,)),
            dma((2,)),
            dma,
            dma((16,)),
            dma((2,)),
            dma((2,)),
            pltpu.SemaphoreType.REGULAR,
            pltpu.SemaphoreType.REGULAR,
        ],
        compiler_params=pltpu.CompilerParams(
            collective_id=0, has_side_effects=True, vmem_limit_bytes=56 * 1024 * 1024
        ),
        cost_estimate=pl.CostEstimate(flops=4_600_000_000, bytes_accessed=12_000_000, transcendentals=0),
    )(slab, virt_size, jnp.transpose(amplitudes, (1, 0, 2)), integrals)
    return jnp.transpose(out, (1, 0, 2))


def solution(mesh):
    return jax.shard_map(
        per_device,
        mesh=mesh,
        in_specs=(P(None, "grid", "rep"), P(None, "grid", "rep"), P(), P()),
        out_specs=P(None, "grid", "rep"),
        check_vma=False,
    )
```

```python
import jax
import jax.numpy as jnp
from jax import lax
from jax.experimental import pallas as pl
from jax.experimental.pallas import tpu as pltpu
from jax.sharding import PartitionSpec as P

NIRREP = 8
O = 128
RING = 4
K = 3328
Q = 208
ROWS = 13
PAD = 16
QUAD = 4
PIECE = QUAD * PAD
LANES = 256
DEPTH = 256
MAIN = 2816
TAIL = K - MAIN
SPARE = PAD - ROWS
FOLDS = 5
STEPS = 32700.0
LAG = 4
MESH = pl.DeviceIdType.MESH


def encode(value, wide):
    peak = jnp.max(jnp.abs(value), axis=1, keepdims=True)
    level = jnp.ceil(jnp.log2(jnp.maximum(peak, 1e-30)) + 0.01)
    wide[:, :Q] = jnp.round(value * (jnp.exp2(-level) * STEPS))
    wide[:, Q:] = jnp.broadcast_to(level, (value.shape[0], LANES - Q))
    return wide[...].astype(jnp.int32).astype(jnp.int16)


def decode(coded):
    value = coded.astype(jnp.int32).astype(jnp.float32)
    return value * (jnp.exp2(value[:, Q:Q + 1]) * (1.0 / STEPS))


def kernel(
    slab_ref, virt_ref, amp_ref, w_hbm, out_ref,
    buf, w_ref, fold, tail, wide, stage, inbox, total, final, low_tab, high_tab, edge_tab,
    w_sem, recv_sem, side_sem, side_send, major_send, minor_send, extra_send,
    part_send, part_recv, sum_send, sum_recv, step_sem, far_sem,
):
    g = lax.axis_index("grid")
    r = lax.axis_index("rep")
    c = lax.rem(g, 2)
    zl = lax.rem(lax.div(g, 2), 2)
    x = lax.rem(lax.div(g, 4), RING)
    y = lax.div(g, 16)
    within = lax.rem(g, 16)
    xs = [lax.rem(x + d, RING) for d in range(RING)]
    ys = [lax.rem(y + d, RING) for d in range(RING)]

    def grid_of(yy, xx, zz, cc):
        return ((yy * RING + xx) * 2 + zz) * 2 + cc

    x_up, x_down = grid_of(y, xs[1], zl, c), grid_of(y, xs[3], zl, c)
    y_up, y_down = grid_of(ys[1], x, zl, c), grid_of(ys[3], x, zl, c)
    sibling = grid_of(y, x, zl, 1 - c)
    partner = grid_of(y, x, 1 - zl, c)
    beyond = (grid_of(y, x, 1 - zl, c), lax.rem(r + 2 * zl + 3, 4))
    minor_up, minor_down = (x_up, y_up), (x_down, y_down)
    major_up, major_down = (y_up, x_up), (y_down, x_down)
    mine = y * RING + x

    barrier = pltpu.get_barrier_semaphore()
    near = [sibling, partner, x_up, x_down, y_up, y_down]
    for n in near:
        pl.semaphore_signal(barrier, inc=1, device_id=(n, r), device_id_type=MESH)
    pl.semaphore_signal(barrier, inc=1, device_id=beyond, device_id_type=MESH)

    w_copy = pltpu.make_async_copy(w_hbm, w_ref, w_sem)
    w_copy.start()
    for m in range(2):
        whole = amp_ref[:, m, :].astype(jnp.float32)
        fold[:ROWS, :] = whole[:, :MAIN]
        fold[ROWS:, FOLDS * TAIL:] = jnp.zeros((SPARE, MAIN - FOLDS * TAIL), jnp.float32)
        fold[ROWS + 1:, (FOLDS - 1) * TAIL:FOLDS * TAIL] = jnp.zeros((SPARE - 1, TAIL), jnp.float32)
        for j in range(FOLDS):
            n = min(SPARE, ROWS - SPARE * j)
            fold[ROWS:ROWS + n, j * TAIL:(j + 1) * TAIL] = whole[SPARE * j:SPARE * j + n, MAIN:]
        buf[m, mine, c * 2 + zl] = fold[...].astype(jnp.bfloat16)
    tail[...] = jnp.zeros_like(tail)

    def table(pos, _):
        first = pos * (QUAD * ROWS)
        last = first + QUAD * ROWS - 1
        low = jnp.int32(-1)
        high = jnp.int32(-1)
        offset = jnp.int32(0)
        edge = jnp.int32(0)
        for h in range(NIRREP):
            low = low + (offset <= first).astype(jnp.int32)
            high = high + (offset <= last).astype(jnp.int32)
            edge = jnp.where(offset <= last, offset, edge)
            offset = offset + virt_ref[h]
        low_tab[pos] = low
        high_tab[pos] = high
        edge_tab[pos] = edge - first
        return 0

    lax.fori_loop(0, 16, table, 0)
    occ = [slab_ref[m] // (O // NIRREP) for m in range(2)]

    pl.semaphore_wait(barrier, len(near) + 1)

    def block_copy(m, pos, z, send, recv, target):
        block = buf.at[m, pos, pl.ds(2 * c, 2)] if z is None else buf.at[m, pos, c * 2 + z]
        return pltpu.make_async_remote_copy(
            src_ref=block, dst_ref=block, send_sem=send, recv_sem=recv,
            device_id=(target, r), device_id_type=MESH,
        )

    def push(m, pos, z, sem, target):
        block_copy(m, pos, z, sem.at[m], recv_sem.at[m, pos], target).start()

    def cross(m, pos):
        block_copy(m, pos, None, side_send.at[m], side_sem.at[m, pos], sibling).start()

    def arrived(m, pos, z):
        block_copy(m, pos, z, side_send.at[m], recv_sem.at[m, pos], sibling).wait_recv()

    def spread(m, pos, z):
        push(m, pos, z, major_send, major_up[m])
        push(m, pos, z, major_send, major_down[m])

    def place(m, tb, ta):
        db, da = (y, x) if m == 0 else (x, y)
        pb, pa = lax.rem(db + tb, RING), lax.rem(da + ta, RING)
        return (pb, pa) if m == 0 else (pa, pb)

    def take(m, tb, ta):
        yy, xx = place(m, tb, ta)
        pos = yy * RING + xx
        arrived(m, pos, None)

        @pl.when(tb == 0)
        def _():
            @pl.when(ta == 1)
            def _():
                push(m, pos, 0, extra_send, minor_down[m])

            @pl.when(ta == 3)
            def _():
                push(m, pos, 1, extra_send, minor_up[m])

            spread(m, pos, None)

        for side, target in ((1, major_down[m]), (3, major_up[m])):
            @pl.when((tb == side) & ((ta == 0) | (ta == 2)))
            def _():
                push(m, pos, side // 2, major_send, target)

            @pl.when((tb == side) & (ta == side))
            def _():
                push(m, pos, None, major_send, target)

        cross(m, pos)

    for m in range(2):
        push(m, mine, zl, extra_send, partner)
    for m in range(2):
        push(m, mine, zl, minor_send, minor_up[m])
        push(m, mine, zl, minor_send, minor_down[m])
        spread(m, mine, zl)
    pl.semaphore_signal(step_sem, inc=1, device_id=(partner, r), device_id_type=MESH)
    pl.semaphore_signal(step_sem, inc=1, device_id=beyond, device_id_type=MESH)
    for m in range(2):
        arrived(m, mine, 1 - zl)
        push(m, mine, 1 - zl, minor_send, minor_up[m])
        push(m, mine, 1 - zl, minor_send, minor_down[m])
        spread(m, mine, 1 - zl)
        cross(m, mine)
    pl.semaphore_wait(step_sem, 2)
    for d in (1, 3):
        pl.semaphore_signal(far_sem, inc=1, device_id=(g, lax.rem(r + d, 4)), device_id_type=MESH)
    w_copy.wait()
    pl.semaphore_wait(far_sem, 2)

    row = lax.broadcasted_iota(jnp.int32, (PIECE, 1), 0)
    part = row // PAD
    row_a = ((part % 2) * 2 + part // 2) * ROWS + row % PAD

    def part_copy(m, pos, yy, xx):
        return pltpu.make_async_remote_copy(
            src_ref=stage.at[m, pos], dst_ref=inbox.at[m, xx, r],
            send_sem=part_send.at[m], recv_sem=part_recv.at[m, xx],
            device_id=(g, yy), device_id_type=MESH,
        )

    def compute(m, tb, ta):
        yy, xx = place(m, tb, ta)
        pos = yy * RING + xx
        pair = buf.at[m, pos, pl.ds(0, 2)]
        pltpu.make_async_remote_copy(
            src_ref=pair, dst_ref=pair, send_sem=side_send.at[m], recv_sem=side_sem.at[m, pos],
            device_id=(sibling, r), device_id_type=MESH,
        ).wait_recv()
        pair_low = low_tab[pos] ^ occ[m]
        pair_high = high_tab[pos] ^ occ[m]
        edge = edge_tab[pos]
        for s in range(QUAD):
            spill = buf[m, pos, s, :, :FOLDS * TAIL].astype(jnp.float32)
            for j in range(FOLDS):
                n = min(SPARE, ROWS - SPARE * j)
                start = s * PAD + SPARE * j
                tail[start:start + n, :] = spill[ROWS:ROWS + n, j * TAIL:(j + 1) * TAIL]
        acc_low = jnp.zeros((PIECE, Q), jnp.float32)
        acc_high = jnp.zeros((PIECE, Q), jnp.float32)
        for k in range(0, K, DEPTH):
            if k < MAIN:
                left = buf[m, pos, :, :, k:k + DEPTH].reshape(PIECE, DEPTH)
            else:
                left = tail[:, k - MAIN:k - MAIN + DEPTH].astype(jnp.bfloat16)
            for which in range(2):
                right = w_ref[pair_high if which else pair_low, :, k:k + DEPTH]
                term = lax.dot_general(left, right, (((1,), (1,)), ((), ())), preferred_element_type=jnp.float32)
                if which:
                    acc_high = acc_high + term
                else:
                    acc_low = acc_low + term
        stage[m, pos] = encode(jnp.where(row_a >= edge, acc_high, acc_low), wide)

        @pl.when(yy != r)
        def _():
            part_copy(m, pos, yy, xx).start()

    def seat(s):
        return lax.rem(s, 2) * 2 + lax.div(s, 2)

    def sum_copy(m, xx, s):
        return pltpu.make_async_remote_copy(
            src_ref=total.at[m, xx, pl.ds(s * PAD, PAD)], dst_ref=final.at[m, within],
            send_sem=sum_send.at[m, xx], recv_sem=sum_recv.at[m],
            device_id=((r * RING + xx) * 4 + seat(s), y), device_id_type=MESH,
        )

    def reduce(m, tb, ta):
        yy, xx = place(m, tb, ta)

        @pl.when(yy == r)
        def _():
            three = inbox.at[m, xx, pl.ds(0, 3)]
            pltpu.make_async_remote_copy(
                src_ref=three, dst_ref=three, send_sem=part_send.at[m], recv_sem=part_recv.at[m, xx],
                device_id=(g, lax.rem(r + 1, 4)), device_id_type=MESH,
            ).wait_recv()
            value = decode(stage[m, yy * RING + xx])
            for d in (1, 2, 3):
                value = value + decode(inbox[m, xx, lax.rem(r + d, 4)])
            total[m, xx] = encode(value[:, :Q], wide)

            def ship(s, _):
                here = (y == r) & ((r * RING + xx) * 4 + seat(s) == g)

                @pl.when(here)
                def _():
                    final[m, within] = total[m, xx, pl.ds(pl.multiple_of(s * PAD, PAD), PAD)]

                @pl.when(jnp.logical_not(here))
                def _():
                    sum_copy(m, xx, s).start()
                return 0

            lax.fori_loop(0, QUAD, ship, 0)

    order = (
        (0, 0), (0, 1), (0, 3), (1, 0), (3, 0), (0, 2), (2, 0), (1, 1),
        (3, 3), (1, 3), (3, 1), (1, 2), (3, 2), (2, 1), (2, 3), (2, 2),
    )

    def code(k, first, last):
        return sum(order[i][k] * 4 ** (i - first) for i in range(first, last))

    def work(step, state):
        tb, ta, cb, ca = state
        nb, na = lax.rem(cb, 4), lax.rem(ca, 4)
        for m in range(2):
            take(m, nb, na)
            compute(m, tb, ta)
        return nb, na, lax.div(cb, 4), lax.div(ca, 4)

    def work_and_reduce(step, states):
        state, (rb, ra) = states
        state = work(step, state)
        for m in range(2):
            reduce(m, lax.rem(rb, 4), lax.rem(ra, 4))
        return state, (lax.div(rb, 4), lax.div(ra, 4))

    def rest(step, old):
        rb, ra = old
        for m in range(2):
            reduce(m, lax.rem(rb, 4), lax.rem(ra, 4))
        return lax.div(rb, 4), lax.div(ra, 4)

    zero = jnp.int32(0)
    state = (zero, zero, jnp.int32(code(0, 1, 16)), jnp.int32(code(1, 1, 16)))
    old = (jnp.int32(code(0, 0, 15 - LAG)), jnp.int32(code(1, 0, 15 - LAG)))
    state = lax.fori_loop(0, LAG, work, state)
    state, _ = lax.fori_loop(LAG, 15, work_and_reduce, (state, old))
    for m in range(2):
        compute(m, state[0], state[1])
    left = (jnp.int32(code(0, 15 - LAG, 16)), jnp.int32(code(1, 15 - LAG, 16)))
    lax.fori_loop(15 - LAG, 16, rest, left)

    def wait_sent(ref, sem):
        pltpu.make_async_remote_copy(
            src_ref=ref, dst_ref=ref, send_sem=sem, recv_sem=sum_recv.at[0],
            device_id=(sibling, r), device_id_type=MESH,
        ).wait_send()

    for m in range(2):
        wait_sent(stage.at[m, pl.ds(0, 12)], part_send.at[m])
        wait_sent(buf.at[m, pl.ds(0, 8)], side_send.at[m])
        wait_sent(buf.at[m, pl.ds(0, 6)], major_send.at[m])
        wait_sent(buf.at[m, 0], minor_send.at[m])
        wait_sent(buf.at[m, 0, pl.ds(0, 3)], extra_send.at[m])
        for xx in range(RING):
            inside = (y == r) & (x == xx)

            @pl.when(inside)
            def _():
                wait_sent(total.at[m, xx, pl.ds(0, PIECE - PAD)], sum_send.at[m, xx])

            @pl.when(jnp.logical_not(inside))
            def _():
                wait_sent(total.at[m, xx], sum_send.at[m, xx])

        def landed(ref):
            pltpu.make_async_remote_copy(
                src_ref=ref, dst_ref=ref, send_sem=sum_send.at[m, 0], recv_sem=sum_recv.at[m],
                device_id=(sibling, r), device_id_type=MESH,
            ).wait_recv()

        @pl.when(y == r)
        def _():
            landed(final.at[m, pl.ds(0, 15)])

        @pl.when(y != r)
        def _():
            landed(final.at[m])
        for k in range(16):
            out_ref[:, m, k * Q:(k + 1) * Q] = decode(final[m, k])[:ROWS, :Q]


def per_device(amplitudes, integrals, virt_size, slab):
    smem = pl.BlockSpec(memory_space=pltpu.SMEM)
    vmem = pl.BlockSpec(memory_space=pltpu.VMEM)
    dma = pltpu.SemaphoreType.DMA
    out = pl.pallas_call(
        kernel,
        out_shape=jax.ShapeDtypeStruct((ROWS, 2, K), jnp.float32),
        in_specs=[smem, smem, vmem, pl.BlockSpec(memory_space=pl.ANY)],
        out_specs=vmem,
        scratch_shapes=[
            pltpu.VMEM((2, 16, QUAD, PAD, MAIN), jnp.bfloat16),
            pltpu.VMEM((NIRREP, Q, K), jnp.bfloat16),
            pltpu.VMEM((PAD, MAIN), jnp.float32),
            pltpu.VMEM((PIECE, TAIL), jnp.float32),
            pltpu.VMEM((PIECE, LANES), jnp.float32),
            pltpu.VMEM((2, 16, PIECE, LANES), jnp.int16),
            pltpu.VMEM((2, 4, 4, PIECE, LANES), jnp.int16),
            pltpu.VMEM((2, 4, PIECE, LANES), jnp.int16),
            pltpu.VMEM((2, 16, PAD, LANES), jnp.int16),
            pltpu.SMEM((16,), jnp.int32),
            pltpu.SMEM((16,), jnp.int32),
            pltpu.SMEM((16,), jnp.int32),
            dma,
            dma((2, 16)),
            dma((2, 16)),
            dma((2,)),
            dma((2,)),
            dma((2,)),
            dma((2,)),
            dma((2,)),
            dma((2, 4)),
            dma((2, 4)),
            dma((2,)),
            pltpu.SemaphoreType.REGULAR,
            pltpu.SemaphoreType.REGULAR,
        ],
        compiler_params=pltpu.CompilerParams(
            collective_id=0, has_side_effects=True, vmem_limit_bytes=56 * 1024 * 1024
        ),
        cost_estimate=pl.CostEstimate(flops=4_600_000_000, bytes_accessed=12_000_000, transcendentals=0),
    )(slab, virt_size, jnp.transpose(amplitudes, (1, 0, 2)), integrals)
    return jnp.transpose(out, (1, 0, 2))


def solution(mesh):
    return jax.shard_map(
        per_device,
        mesh=mesh,
        in_specs=(P(None, "grid", "rep"), P(None, "grid", "rep"), P(), P()),
        out_specs=P(None, "grid", "rep"),
        check_vma=False,
    )
```
